32 devices in a mesh: dp: 8 (over y, x, core), tensor: 4 (over z).
Axes of the slice: x: 2, y: 2, z: 4, core: 2. Of those that a mesh axis runs over, the one named last changes fastest.
Arguments:
- kv_cache: bfloat16 [64, 512, 2048], P('dp', None, 'tensor'), may hold values from -4 to 4
- new_kv: bfloat16 [4, 64, 2048], P(None, 'dp', 'tensor'), may hold values from -4 to 4
- queries: bfloat16 [4, 64, 8192], P(None, 'dp', 'tensor'), may hold values from -80 to 80
- verify_q: bfloat16 [16, 512, 8192], P('dp', None, 'tensor'), may hold values from -80 to 80
- prompt_kv: bfloat16 [8, 256, 2048], P('dp', None, 'tensor'), may hold values from -4 to 4
- readout: bfloat16 [8192], P('tensor'), may hold values from -0.1875 to 0.1875
- finish: int32 [64], replicated, may hold values from 0 to 4, as said below
- dest: int32 [64], replicated, may hold values from -1 to 15, as said below
- prompt: int32 [64], replicated, may hold values from -1 to 7, as said below
- lengths: int32 [64], replicated, may hold values from 2 to 508
Outputs:
- decoded: bfloat16 [4, 64, 8192], P(None, 'dp', 'tensor')
- new_cache: bfloat16 [64, 512, 2048], P('dp', None, 'tensor')
- rewards: float32 [16, 512], P('dp', 'tensor')
The draws below stay inside these ranges and needn't reach their ends.
Inputs may be any that keep to these rules, and one draw needn't show every extreme that they name: 4 marks a row that does not finish; rows with a smaller value are finished candidates; at most 2 rows of one dp index finish, and in every draw some dp index has exactly 2 finished rows. `dest`: -1 exactly for rows that do not finish; no verifier slot receives two rows; the finished rows of one dp index go to slots of distinct dp indices; in every draw some dp index has all 2 of its slots filled. `prompt`: -1 exactly for rows that do not finish.
All inputs are finite; a program needn't handle non-finite values.
Results may differ from the reference program's by a relative error of at most 0.007.
Values may be sent and summed in bfloat16 or wider, within the bound.
A program may use at most 192 MiB of HBM per device.

```python
import math
import jax
import jax.numpy as jnp
from jax import lax

KVH = 8
GROUP = 8
D_HEAD = 128
ROWS = 8
CTX = 512
PLEN = 256
STEPS = 4
VSLOTS = 2
HALF = 64
HEADS = 64
ROWS_ALL = 64
VTOTAL = 16
PROMPTS = 8


def routing(key):
    key = jax.random.fold_in(key, 77)
    devices = ROWS_ALL // ROWS
    key_list = jax.random.split(key, 10)
    outer_perm = jax.random.permutation(key_list[0], devices)
    inner_perm = jax.random.permutation(key_list[1], devices)
    shifts = jax.random.permutation(key_list[2], devices)[:VSLOTS]
    target = outer_perm[(inner_perm[:, None] + shifts[None, :]) % devices]
    rate_level = jax.random.randint(key_list[3], (devices, 1), 0, 5)
    coin_draw = jax.random.randint(key_list[4], (devices, VSLOTS), 0, 4)
    full_device = jax.random.randint(key_list[5], (), 0, devices)
    full_source = jax.random.randint(jax.random.fold_in(key_list[5], 1), (), 0, devices)
    finished = (coin_draw < rate_level) | (target == full_device) | (jnp.arange(devices)[:, None] == full_source)
    row_order = jax.vmap(lambda sub_key: jax.random.permutation(sub_key, ROWS))(jax.random.split(key_list[6], devices))[:, :VSLOTS]
    row_ids = (jnp.arange(devices)[:, None] * ROWS + row_order).reshape(-1)
    slot_ids = (target * VSLOTS + jnp.arange(VSLOTS)[None, :]).reshape(-1)
    step_ids = jax.random.randint(key_list[7], (devices, VSLOTS), 0, STEPS).reshape(-1)
    prompt_ids = jax.random.randint(key_list[8], (devices, VSLOTS), 0, PROMPTS).reshape(-1)
    finished_flat = finished.reshape(-1)
    finish = jnp.full((ROWS_ALL,), STEPS, jnp.int32).at[row_ids].set(jnp.where(finished_flat, step_ids, STEPS).astype(jnp.int32))
    dest = jnp.full((ROWS_ALL,), -1, jnp.int32).at[row_ids].set(jnp.where(finished_flat, slot_ids, -1).astype(jnp.int32))
    prompt = jnp.full((ROWS_ALL,), -1, jnp.int32).at[row_ids].set(jnp.where(finished_flat, prompt_ids, -1).astype(jnp.int32))
    lengths = jax.random.randint(key_list[9], (ROWS_ALL,), 2, CTX - STEPS + 1)
    longest = jax.random.randint(jax.random.fold_in(key_list[9], 1), (), 0, ROWS_ALL)
    lengths = lengths.at[longest].set(CTX - STEPS).astype(jnp.int32)
    return (finish, dest, prompt, lengths)


def cache_base(key):
    key = jax.random.fold_in(key, 91)
    cache_draw = jax.random.truncated_normal(key, -4.0, 4.0, (ROWS_ALL, CTX, 2, KVH, 2, HALF), jnp.float32)
    tied_keys = cache_draw[:, 1, :, :, 0, :]
    return cache_draw.at[:, 1, :, :, 0, :].set(tied_keys)


def draw_finish(key, part):
    routes = routing(key)
    return routes[0]


def draw_dest(key, part):
    routes = routing(key)
    return routes[1]


def draw_prompt(key, part):
    routes = routing(key)
    return routes[2]


def draw_lengths(key, part):
    routes = routing(key)
    return routes[3]


def draw_kv_cache(key, part):
    cache_draw = cache_base(key)
    return cache_draw.reshape(ROWS_ALL, CTX, 4 * KVH * HALF).astype(jnp.bfloat16)


def draw_queries(key, part):
    aligned_share = 0.0
    cache_draw = cache_base(key)
    key = jax.random.fold_in(key, 6)
    key_list = jax.random.split(key, 3)
    noise_draw = jax.random.truncated_normal(key_list[0], -4.0, 4.0, (STEPS, ROWS_ALL, 2, KVH, GROUP, HALF), jnp.float32)
    first_keys = cache_draw[:, 0, :, :, 0, :]
    aligned_mask = jax.random.uniform(key_list[1], (STEPS, ROWS_ALL, 1, 1, 1, 1)) < aligned_share
    strength = 9.0 + 11.0 * jax.random.uniform(key_list[2], (STEPS, ROWS_ALL, 1, 1, 1, 1))
    aligned = strength * first_keys[None, :, :, :, None, :]
    values = jnp.where(aligned_mask, aligned, noise_draw)
    return values.reshape(STEPS, ROWS_ALL, 2 * KVH * GROUP * HALF).astype(jnp.bfloat16)


def draw_verify_q(key, part):
    aligned_share = 0.0
    cache_draw = cache_base(key)
    routes = routing(key)
    key = jax.random.fold_in(key, 7)
    key_list = jax.random.split(key, 3)
    slot_match = routes[1][None, :] == jnp.arange(VTOTAL)[:, None]
    source = jnp.sum(jnp.where(slot_match, jnp.arange(ROWS_ALL)[None, :], 0), axis=1)
    first_keys = cache_draw[source, 0, :, :, 0, :]
    noise_draw = jax.random.truncated_normal(key_list[0], -4.0, 4.0, (VTOTAL, CTX, 2, KVH, GROUP, HALF), jnp.float32)
    later = (jnp.arange(CTX) >= 1)[None, :, None, None, None, None]
    aligned_mask = (jax.random.uniform(key_list[1], (VTOTAL, CTX, 1, 1, 1, 1)) < aligned_share) & later
    strength = 9.0 + 11.0 * jax.random.uniform(key_list[2], (VTOTAL, CTX, 1, 1, 1, 1))
    aligned = strength * first_keys[:, None, :, :, None, :]
    values = jnp.where(aligned_mask, aligned, noise_draw)
    return values.reshape(VTOTAL, CTX, 2 * KVH * GROUP * HALF).astype(jnp.bfloat16)


def shard_levels(key, dims, cuts, least, high):
    loudness, own = 1.0, jax.random.fold_in(key, 6)
    for axis_at, shards_of in cuts:
        steps = jnp.exp(jax.random.uniform(jax.random.fold_in(own, axis_at), (shards_of,), jnp.float32, least / len(cuts), high / len(cuts)))
        loudness = loudness * jnp.repeat(steps, dims[axis_at] // shards_of).reshape([-1 if axis == axis_at else 1 for axis in range(len(dims))])
    return loudness


def normal_values(rng, extent, deviation, most, cuts=(), dtype=jnp.bfloat16):
    values = jax.random.normal(rng, extent, jnp.float32) * deviation
    if len(cuts) > 0:
        values = shard_levels(rng, extent, cuts, -0.22, 0.18) * values
    return jnp.clip(values, min=-most, max=most).astype(dtype)


def setup_inputs(seed: int = 0) -> dict:
    keys = jax.random.split(jax.random.key(seed), 11)
    kv_cache = draw_kv_cache(jax.random.fold_in(keys[10], 71), 0)
    new_kv = normal_values(keys[1], (STEPS, ROWS_ALL, 4 * KVH * HALF), 1.0, 4.0, ((1, 8), (2, 4)))
    queries = draw_queries(jax.random.fold_in(keys[10], 71), 0)
    verify_q = draw_verify_q(jax.random.fold_in(keys[10], 71), 0)
    prompt_kv = normal_values(keys[4], (PROMPTS, PLEN, 4 * KVH * HALF), 1.0, 4.0, ((0, 8), (2, 4)))
    readout = normal_values(keys[5], (HEADS * D_HEAD,), (KVH * D_HEAD) ** -0.5, 0.1875, ((0, 4),))
    finish = draw_finish(jax.random.fold_in(keys[10], 71), 0)
    dest = draw_dest(jax.random.fold_in(keys[10], 71), 0)
    prompt = draw_prompt(jax.random.fold_in(keys[10], 71), 0)
    lengths = draw_lengths(jax.random.fold_in(keys[10], 71), 0)
    return dict(kv_cache=kv_cache, new_kv=new_kv, queries=queries, verify_q=verify_q, prompt_kv=prompt_kv, readout=readout, finish=finish, dest=dest, prompt=prompt, lengths=lengths)


def query_heads(flat_cols):
    lead_dims = flat_cols.shape[:-1]
    shaped = flat_cols.reshape(lead_dims + (2, KVH, GROUP, HALF))
    moved_axes = jnp.moveaxis(shaped, -4, -2)
    return moved_axes.reshape(lead_dims + (KVH, GROUP, D_HEAD))

def query_columns(heads):
    lead_dims = heads.shape[:-3]
    shaped = heads.reshape(lead_dims + (KVH, GROUP, 2, HALF))
    moved_axes = jnp.moveaxis(shaped, -2, -4)
    return moved_axes.reshape(lead_dims + (2 * KVH * GROUP * HALF,))

def key_value(flat_cols):
    lead_dims = flat_cols.shape[:-1]
    shaped = flat_cols.reshape(lead_dims + (2, KVH, 2, HALF))
    key_part = jnp.moveaxis(shaped[..., 0, :], -3, -2).reshape(lead_dims + (KVH, D_HEAD))
    value_part = jnp.moveaxis(shaped[..., 1, :], -3, -2).reshape(lead_dims + (KVH, D_HEAD))
    return (key_part, value_part)

def reference(kv_cache, new_kv, queries, verify_q, prompt_kv, readout, finish, dest, prompt, lengths):
    score_scale = 1.0 / math.sqrt(D_HEAD)
    steps_seen = jnp.arange(STEPS)
    position = jnp.arange(CTX)
    final_cache = kv_cache
    for step_index in range(STEPS):
        hit_mask = (position[None, :] == lengths[:, None] + step_index) & (step_index <= finish[:, None])
        final_cache = jnp.where(hit_mask[:, :, None], new_kv[step_index][:, None, :], final_cache)
    keys_old, values_old = key_value(kv_cache)
    keys_new, values_new = key_value(new_kv)
    query_full = query_heads(queries).astype(jnp.float32)
    score_old = jnp.einsum('srhgd,rphd->srhgp', query_full, keys_old.astype(jnp.float32)) * score_scale
    score_new = jnp.einsum('srhgd,trhd->srhgt', query_full, keys_new.astype(jnp.float32)) * score_scale
    old_valid = (position[None, :] < lengths[:, None])[None, :, None, None, :]
    new_valid = (steps_seen[None, :] <= steps_seen[:, None])[:, None, None, None, :]
    score_old = jnp.where(old_valid, score_old, -jnp.inf)
    score_new = jnp.where(new_valid, score_new, -jnp.inf)
    row_top = jnp.maximum(lax.optimization_barrier(jnp.max(score_old, axis=-1, keepdims=True)), lax.optimization_barrier(jnp.max(score_new, axis=-1, keepdims=True)))
    exp_old = jnp.exp(score_old - row_top)
    exp_new = jnp.exp(score_new - row_top)
    exp_total = lax.optimization_barrier(jnp.sum(exp_old, axis=-1, keepdims=True)) + lax.optimization_barrier(jnp.sum(exp_new, axis=-1, keepdims=True))
    prob_old = (exp_old / exp_total).astype(jnp.bfloat16)
    prob_new = (exp_new / exp_total).astype(jnp.bfloat16)
    mixed_out = jnp.einsum('srhgp,rphd->srhgd', prob_old.astype(jnp.float32), values_old.astype(jnp.float32))
    mixed_out = mixed_out + jnp.einsum('srhgt,trhd->srhgd', prob_new.astype(jnp.float32), values_new.astype(jnp.float32))
    live_step = (steps_seen[:, None] <= finish[None, :])[:, :, None, None, None]
    mixed_out = jnp.where(live_step, mixed_out, 0.0)
    decoded = query_columns(mixed_out).astype(jnp.bfloat16)
    slot_match = dest[None, :] == jnp.arange(VTOTAL)[:, None]
    source = lax.optimization_barrier(jnp.sum(jnp.where(slot_match, jnp.arange(ROWS_ALL)[None, :], 0), axis=1)).astype(jnp.int32)
    span_len = lax.optimization_barrier(jnp.sum(jnp.where(slot_match, (lengths + finish + 1)[None, :], 0), axis=1)).astype(jnp.int32)
    weight_heads = query_heads(readout).astype(jnp.float32)
    query_pos = jnp.arange(CTX)[:, None]
    key_pos = jnp.arange(CTX)[None, :]

    def one_slot(arguments):
        flat_query, row_id, slot_span = arguments
        slot_query = query_heads(flat_query).astype(jnp.float32)
        key_part, value_part = key_value(final_cache[row_id])
        scores = jnp.einsum('thgd,phd->hgtp', slot_query, key_part.astype(jnp.float32)) * score_scale
        allowed = (key_pos <= query_pos) & (key_pos < jnp.maximum(slot_span, 1))
        scores = jnp.where(allowed, scores, -jnp.inf)
        slot_top = lax.optimization_barrier(jnp.max(scores, axis=-1, keepdims=True))
        exp_scores = jnp.exp(scores - slot_top)
        prob_weights = (exp_scores / lax.optimization_barrier(jnp.sum(exp_scores, axis=-1, keepdims=True))).astype(jnp.bfloat16)
        attended = jnp.einsum('hgtp,phd->thgd', prob_weights.astype(jnp.float32), value_part.astype(jnp.float32))
        reward_row = jnp.einsum('thgd,hgd->t', attended, weight_heads, precision=lax.Precision.HIGHEST)
        return jnp.where(jnp.arange(CTX) < slot_span, reward_row, 0.0)
    rewards = lax.map(one_slot, (verify_q, source, span_len))
    picked = prompt_kv[jnp.maximum(prompt, 0)]
    padded = jnp.concatenate([picked, jnp.zeros((ROWS_ALL, CTX - PLEN, picked.shape[2]), jnp.bfloat16)], axis=1)
    new_cache = jnp.where((finish < STEPS)[:, None, None], padded, final_cache)
    return (decoded, new_cache, rewards)
```

```python
import functools
import math

import jax
import jax.numpy as jnp
from jax import lax
from jax.experimental import pallas as pl
from jax.experimental.pallas import tpu as pltpu
from jax.sharding import PartitionSpec as P

GROUP = 8
D_HEAD = 128
HALF = 64
SCALE = 1.0 / math.sqrt(D_HEAD)
NT = (((1,), (1,)), ((), ()))


def from_partner(value, axis, apart):
    mask = 2**apart
    pairs = [(source, source ^ mask) for source in range(lax.axis_size(axis))]
    return lax.ppermute(value, axis, pairs)


def partial_kernel(heads, meta_ref, q_ref, kv_ref, out_ref):
    del meta_ref
    for h in range(heads):
        tile = kv_ref[0, :, h * D_HEAD : (h + 1) * D_HEAD]
        out_ref[0, h] = lax.dot_general(q_ref[0, h], tile, NT, preferred_element_type=jnp.float32)


def soft_kernel(heads, meta_ref, q_ref, kv_ref, other_ref, weight_ref, out_ref):
    row = meta_ref[0] + pl.program_id(0)
    length = meta_ref[1 + row]
    shape = other_ref.shape[2:]
    step = lax.broadcasted_iota(jnp.int32, shape, 0) // GROUP
    seen = lax.broadcasted_iota(jnp.int32, shape, 1) <= length + step
    for h in range(heads):
        tile = kv_ref[0, :, h * D_HEAD : (h + 1) * D_HEAD]
        mine = lax.dot_general(q_ref[0, h], tile, NT, preferred_element_type=jnp.float32)
        score = jnp.where(seen, (mine + other_ref[0, h]) * SCALE, -jnp.inf)
        score = jnp.exp(score - jnp.max(score, axis=-1, keepdims=True))
        weight = (score / jnp.sum(score, axis=-1, keepdims=True)).astype(jnp.bfloat16)
        weight_ref[0, h] = weight
        out_ref[0, h] = jnp.dot(weight, tile, preferred_element_type=jnp.float32)


def value_kernel(heads, meta_ref, weight_ref, kv_ref, out_ref):
    del meta_ref
    for h in range(heads):
        tile = kv_ref[0, :, h * D_HEAD : (h + 1) * D_HEAD]
        out_ref[0, h] = jnp.dot(weight_ref[0, h], tile, preferred_element_type=jnp.float32)


def row_call(kernel, meta, operands, kinds, out_kinds, rows, flops):
    def spec(shape, kind):
        tail = (0,) * (len(shape) - 1)
        if kind == "all":
            return pl.BlockSpec((1,) + shape[1:], lambda i, meta: (meta[0] + i,) + tail)
        return pl.BlockSpec((1,) + shape[1:], lambda i, meta: (i,) + tail)

    return pl.pallas_call(
        kernel,
        out_shape=out_kinds,
        grid_spec=pltpu.PrefetchScalarGridSpec(
            num_scalar_prefetch=1,
            grid=(rows,),
            in_specs=[spec(x.shape, k) for x, k in zip(operands, kinds)],
            out_specs=[spec(x.shape, "half") for x in out_kinds],
        ),
        cost_estimate=pl.CostEstimate(flops=flops, bytes_accessed=4 << 20, transcendentals=1 << 18),
    )(meta, *operands)


def verify_kernel(block, span_ref, qm_ref, qo_ref, key_ref, u_ref, out_ref):
    @pl.when(pl.program_id(0) == 0)
    def _():
        out_ref[...] = jnp.zeros_like(out_ref)

    span = span_ref[0]
    for tb in range(qm_ref.shape[0] // block):
        low, high = tb * block, (tb + 1) * block

        @pl.when(span > low)
        def _():
            query = jnp.concatenate([qm_ref[low:high], qo_ref[low:high]], axis=1)
            t = lax.broadcasted_iota(jnp.int32, (block, high), 0) + low
            p = lax.broadcasted_iota(jnp.int32, (block, high), 1)
            allowed = (p <= t) & (p < jnp.maximum(span, 1))
            total = jnp.zeros((block, 1), jnp.float32)
            for g in range(2):
                score = lax.dot_general(
                    query, key_ref[0, g, :high], NT, preferred_element_type=jnp.float32
                )
                score = jnp.where(allowed, score, -jnp.inf)
                top = jnp.max(score, axis=-1, keepdims=True)
                grown = jnp.exp2((score - top) * (SCALE * math.log2(math.e)))
                weighed = jnp.sum(grown * u_ref[0, g : g + 1, :high], axis=-1, keepdims=True)
                total += weighed / jnp.sum(grown, axis=-1, keepdims=True)
            out_ref[low:high] += jnp.broadcast_to(total, (block, 128))


def verify_call(span, q_mine, q_other, keys, u_pairs):
    context_len = q_mine.shape[0]
    pairs = u_pairs.shape[0]
    per_head = pairs // keys.shape[0]
    return pl.pallas_call(
        functools.partial(verify_kernel, 128),
        out_shape=jax.ShapeDtypeStruct((context_len, 128), jnp.float32),
        grid_spec=pltpu.PrefetchScalarGridSpec(
            num_scalar_prefetch=1,
            grid=(pairs,),
            in_specs=[
                pl.BlockSpec((context_len, 128), lambda i, s: (0, i)),
                pl.BlockSpec((context_len, 128), lambda i, s: (0, i)),
                pl.BlockSpec((1,) + keys.shape[1:], lambda i, s: (i // per_head, 0, 0, 0)),
                pl.BlockSpec((1, 2, context_len), lambda i, s: (i, 0, 0)),
            ],
            out_specs=pl.BlockSpec((context_len, 128), lambda i, s: (0, 0)),
        ),
        compiler_params=pltpu.CompilerParams(vmem_limit_bytes=24 << 20),
        cost_estimate=pl.CostEstimate(
            flops=pairs * 8 * context_len * context_len * D_HEAD,
            bytes_accessed=8 << 20,
            transcendentals=pairs * context_len * context_len,
        ),
    )(span, q_mine, q_other, keys, u_pairs)


def body(kv_cache, new_kv, queries, verify_q, prompt_kv, readout, finish, dest, prompt, lengths):
    row_count, context_len, columns = kv_cache.shape
    step_count = new_kv.shape[0]
    slot_count = verify_q.shape[0]
    plen = prompt_kv.shape[1]
    kv_local = columns // (2 * HALF)
    tp_size = lax.axis_size("tensor")
    peer_count = lax.axis_size("dp")
    my_index = lax.axis_index("dp")
    side = lax.axis_index("tensor") // (tp_size // 2)
    pair_bit = tp_size.bit_length() - 2
    swap = functools.partial(from_partner, axis="tensor", apart=pair_bit)
    first_row = my_index * row_count
    my_finish = lax.dynamic_slice_in_dim(finish, first_row, row_count)
    my_dest = lax.dynamic_slice_in_dim(dest, first_row, row_count)
    my_prompt = lax.dynamic_slice_in_dim(prompt, first_row, row_count)
    my_length = lax.dynamic_slice_in_dim(lengths, first_row, row_count)

    position = jnp.arange(context_len)
    grown = kv_cache
    for step in range(step_count):
        hit = position[None, :] == my_length[:, None] + step
        grown = jnp.where(hit[:, :, None], new_kv[step][:, None, :], grown)

    half = row_count // 2
    step_queries = step_count * GROUP
    q_rows = queries.reshape(step_count, row_count, kv_local, GROUP, HALF)
    q_rows = q_rows.transpose(1, 2, 0, 3, 4).reshape(row_count, kv_local, step_queries, HALF)
    q_rows = jnp.pad(q_rows, ((0, 0), (0, 0), (0, 0), (0, HALF)))
    keep_meta = jnp.concatenate([(side * half)[None], my_length]).astype(jnp.int32)
    give_meta = jnp.concatenate([((1 - side) * half)[None], my_length]).astype(jnp.int32)
    flops = 2 * half * kv_local * step_queries * context_len * D_HEAD
    score_kind = jax.ShapeDtypeStruct((half, kv_local, step_queries, context_len), jnp.float32)
    weight_kind = jax.ShapeDtypeStruct(score_kind.shape, jnp.bfloat16)
    mixed_kind = jax.ShapeDtypeStruct((half, kv_local, step_queries, D_HEAD), jnp.float32)
    (given,) = row_call(
        functools.partial(partial_kernel, kv_local),
        give_meta, (q_rows, grown), ("all", "all"), [score_kind], half, flops,
    )
    other_part = swap(given)

    per_side = slot_count // 2
    keep_query = lax.dynamic_slice_in_dim(verify_q, side * per_side, per_side)
    other_query = swap(lax.dynamic_slice_in_dim(verify_q, (1 - side) * per_side, per_side))

    finished_row = my_finish < step_count
    rank = jnp.cumsum(finished_row.astype(jnp.int32)) - 1
    weight = readout.reshape(kv_local, GROUP, HALF)
    target = jnp.where(finished_row, my_dest // slot_count, -1)
    key_out = jnp.zeros((), jnp.bfloat16)
    u_out = jnp.zeros((), jnp.float32)
    peers = jnp.arange(peer_count)[:, None, None]
    picks = []
    for turn in range(2):
        is_turn = finished_row & (rank == turn)
        row = jnp.argmax(is_turn)
        goes = jnp.max(jnp.where(is_turn, target, -1))
        picks.append((is_turn, jnp.maximum(my_prompt[row], 0)))
        picked = lax.dynamic_index_in_dim(grown, row, 0, keepdims=False)
        picked = picked.reshape(context_len, kv_local, 2, HALF)
        keys = picked[:, :, 0, :].reshape(context_len, kv_local * HALF)
        u_part = jnp.einsum(
            "phd,hgd->hgp", picked[:, :, 1, :], weight, preferred_element_type=jnp.float32
        ).reshape(kv_local * GROUP, context_len)
        key_out = jnp.where(peers == goes, keys[None], key_out)
        u_out = jnp.where(peers == goes, u_part[None], u_out)
    key_in = lax.all_to_all(key_out, "dp", split_axis=0, concat_axis=0, tiled=True)
    u_in = lax.all_to_all(u_out, "dp", split_axis=0, concat_axis=0, tiled=True)
    wanted = my_index * slot_count + jnp.arange(slot_count)
    slot_hits = dest.reshape(peer_count, row_count)[None] == wanted[:, None, None]
    full_span = (lengths + finish + 1).reshape(peer_count, row_count)
    span_len = jnp.sum(jnp.where(slot_hits, full_span[None], 0), axis=(1, 2))
    source = jnp.argmax(jnp.any(slot_hits, axis=2), axis=1)

    def of_slots(array, first):
        return jnp.stack([
            lax.dynamic_index_in_dim(array, source[first + i], 0, keepdims=False)
            for i in range(per_side)
        ])

    first_keep, first_give = side * per_side, (1 - side) * per_side
    other_keys, other_u = swap((of_slots(key_in, first_give), of_slots(u_in, first_give)))
    keep_keys = of_slots(key_in, first_keep)
    u_full = of_slots(u_in, first_keep) + other_u

    def by_head(keys):
        return keys.reshape(per_side, context_len, kv_local, HALF).transpose(0, 2, 1, 3)

    mine, other = by_head(keep_keys), by_head(other_keys)
    blank = jnp.zeros_like(mine)
    key_pairs = jnp.stack([
        jnp.concatenate([mine, blank, other, blank], axis=-1),
        jnp.concatenate([blank, mine, blank, other], axis=-1),
    ], axis=2)

    weights, mixed_keep = row_call(
        functools.partial(soft_kernel, kv_local),
        keep_meta, (q_rows, grown, other_part), ("all", "all", "half"),
        [weight_kind, mixed_kind], half, 2 * flops,
    )
    other_weights = swap(weights)

    slot_rewards = []
    for i in range(per_side):
        slot_span = span_len[first_keep + i]
        reward = verify_call(
            slot_span[None].astype(jnp.int32), keep_query[i], other_query[i], key_pairs[i],
            u_full[i].reshape(kv_local * GROUP // 2, 2, context_len),
        )[:, 0]
        slot_rewards.append(jnp.where(position < slot_span, reward, 0.0))
    kept = jnp.stack(slot_rewards)
    nothing = jnp.zeros_like(kept)
    partial_value = jnp.concatenate(
        [jnp.where(side == 0, kept, nothing), jnp.where(side == 0, nothing, kept)]
    )
    rewards = lax.psum_scatter(partial_value, "tensor", scatter_dimension=1, tiled=True)

    (mixed_give,) = row_call(
        functools.partial(value_kernel, kv_local),
        give_meta, (other_weights, grown), ("half", "all"), [mixed_kind], half, flops,
    )
    mixed_keep, mixed_give = mixed_keep[..., HALF:], mixed_give[..., HALF:]
    mixed = jnp.concatenate([
        jnp.where(side == 0, mixed_keep, mixed_give), jnp.where(side == 0, mixed_give, mixed_keep)
    ]).reshape(row_count, kv_local, step_count, GROUP, HALF).transpose(2, 0, 1, 3, 4)
    live = jnp.arange(step_count)[:, None] <= my_finish[None, :]
    decoded = jnp.where(live[:, :, None, None, None], mixed, 0.0)
    decoded = decoded.astype(jnp.bfloat16).reshape(queries.shape)

    prompts = lax.all_gather(prompt_kv, "dp", axis=0, tiled=True)
    new_cache = grown
    for is_turn, which in picks:
        refill = lax.dynamic_index_in_dim(prompts, which, 0, keepdims=False)
        refill = jnp.pad(refill, ((0, context_len - plen), (0, 0)))
        new_cache = jnp.where(is_turn[:, None, None], refill[None], new_cache)
    return (decoded, new_cache, rewards)


def solution(mesh):
    placed = (
        P("dp", None, "tensor"),
        P(None, "dp", "tensor"),
        P(None, "dp", "tensor"),
        P("dp", None, "tensor"),
        P("dp", None, "tensor"),
        P("tensor"),
        P(),
        P(),
        P(),
        P(),
    )
    return jax.shard_map(
        body,
        mesh=mesh,
        in_specs=placed,
        out_specs=(P(None, "dp", "tensor"), P("dp", None, "tensor"), P("dp", "tensor")),
        check_vma=False,
    )
```

```python
import functools
import math

import jax
import jax.numpy as jnp
from jax import lax
from jax.experimental import pallas as pl
from jax.experimental.pallas import tpu as pltpu
from jax.sharding import PartitionSpec as P

GROUP = 8
D_HEAD = 128
HALF = 64
SCALE = 1.0 / math.sqrt(D_HEAD)
NT = (((1,), (1,)), ((), ()))


def from_partner(value, axis, apart):
    mask = 2**apart
    pairs = [(source, source ^ mask) for source in range(lax.axis_size(axis))]
    return lax.ppermute(value, axis, pairs)


def partial_kernel(heads, steps, meta_ref, q_ref, kv_ref, new_ref, out_ref):
    length = meta_ref[1 + meta_ref[0] + pl.program_id(0)]
    position = lax.broadcasted_iota(jnp.int32, out_ref.shape[2:], 1)
    for h in range(heads):
        tile = kv_ref[0, :, h * D_HEAD : (h + 1) * D_HEAD]
        fresh = new_ref[0, :, h * D_HEAD : (h + 1) * D_HEAD]
        score = lax.dot_general(q_ref[0, h], tile, NT, preferred_element_type=jnp.float32)
        extra = lax.dot_general(q_ref[0, h], fresh, NT, preferred_element_type=jnp.float32)
        for t in range(steps):
            score = jnp.where(position == length + t, extra[:, t : t + 1], score)
        out_ref[0, h] = score


def soft_kernel(heads, meta_ref, q_ref, kv_ref, other_ref, weight_ref, out_ref):
    row = meta_ref[0] + pl.program_id(0)
    length = meta_ref[1 + row]
    shape = other_ref.shape[2:]
    step = lax.broadcasted_iota(jnp.int32, shape, 0) // GROUP
    seen = lax.broadcasted_iota(jnp.int32, shape, 1) <= length + step
    for h in range(heads):
        tile = kv_ref[0, :, h * D_HEAD : (h + 1) * D_HEAD]
        mine = lax.dot_general(q_ref[0, h], tile, NT, preferred_element_type=jnp.float32)
        score = jnp.where(seen, (mine + other_ref[0, h]) * SCALE, -jnp.inf)
        score = jnp.exp(score - jnp.max(score, axis=-1, keepdims=True))
        weight = (score / jnp.sum(score, axis=-1, keepdims=True)).astype(jnp.bfloat16)
        weight_ref[0, h] = weight
        out_ref[0, h] = jnp.dot(weight, tile, preferred_element_type=jnp.float32)


def value_kernel(heads, meta_ref, weight_ref, kv_ref, out_ref):
    del meta_ref
    for h in range(heads):
        tile = kv_ref[0, :, h * D_HEAD : (h + 1) * D_HEAD]
        out_ref[0, h] = jnp.dot(weight_ref[0, h], tile, preferred_element_type=jnp.float32)


def row_call(kernel, meta, operands, kinds, out_kinds, rows, flops):
    def spec(shape, kind):
        tail = (0,) * (len(shape) - 1)
        if kind == "all":
            return pl.BlockSpec((1,) + shape[1:], lambda i, meta: (meta[0] + i,) + tail)
        return pl.BlockSpec((1,) + shape[1:], lambda i, meta: (i,) + tail)

    return pl.pallas_call(
        kernel,
        out_shape=out_kinds,
        grid_spec=pltpu.PrefetchScalarGridSpec(
            num_scalar_prefetch=1,
            grid=(rows,),
            in_specs=[spec(x.shape, k) for x, k in zip(operands, kinds)],
            out_specs=[spec(x.shape, "half") for x in out_kinds],
        ),
        cost_estimate=pl.CostEstimate(flops=flops, bytes_accessed=4 << 20, transcendentals=1 << 18),
    )(meta, *operands)


def pick_kernel(heads, steps, meta_ref, kv_ref, new_ref, pick_ref, weight_ref, key_ref, u_ref):
    length = meta_ref[2 + pl.program_id(0)]
    position = lax.broadcasted_iota(jnp.int32, key_ref.shape[1:], 0)
    keys = jnp.dot(kv_ref[0], pick_ref[...], preferred_element_type=jnp.float32)
    fresh = jnp.dot(new_ref[0], pick_ref[...], preferred_element_type=jnp.float32)
    for t in range(steps):
        keys = jnp.where(position == length + t, fresh[t : t + 1], keys)
    key_ref[0] = keys.astype(jnp.bfloat16)
    position = lax.broadcasted_iota(jnp.int32, (GROUP, u_ref.shape[2]), 1)
    for h in range(heads):
        at = slice(h * D_HEAD, (h + 1) * D_HEAD)
        u = lax.dot_general(weight_ref[h], kv_ref[0, :, at], NT, preferred_element_type=jnp.float32)
        extra = lax.dot_general(
            weight_ref[h], new_ref[0, :, at], NT, preferred_element_type=jnp.float32
        )
        for t in range(steps):
            u = jnp.where(position == length + t, extra[:, t : t + 1], u)
        u_ref[0, h * GROUP : (h + 1) * GROUP] = u


def pick_call(heads, steps, meta, kv, fresh, picks, weight):
    count, context_len, columns = kv.shape
    kinds = [
        jax.ShapeDtypeStruct((2, context_len, columns // 2), jnp.bfloat16),
        jax.ShapeDtypeStruct((2, heads * GROUP, context_len), jnp.float32),
    ]
    return pl.pallas_call(
        functools.partial(pick_kernel, heads, steps),
        out_shape=kinds,
        grid_spec=pltpu.PrefetchScalarGridSpec(
            num_scalar_prefetch=1,
            grid=(2,),
            in_specs=[
                pl.BlockSpec((1,) + kv.shape[1:], lambda i, meta: (meta[i], 0, 0)),
                pl.BlockSpec((1,) + fresh.shape[1:], lambda i, meta: (meta[i], 0, 0)),
                pl.BlockSpec(picks.shape, lambda i, meta: (0, 0)),
                pl.BlockSpec(weight.shape, lambda i, meta: (0, 0, 0)),
            ],
            out_specs=[pl.BlockSpec((1,) + k.shape[1:], lambda i, meta: (i, 0, 0)) for k in kinds],
        ),
        cost_estimate=pl.CostEstimate(flops=1 << 28, bytes_accessed=2 << 20, transcendentals=0),
    )(meta, kv, fresh, picks, weight)


def verify_kernel(block, span_ref, qm_ref, qo_ref, key_ref, u_ref, out_ref, sums_ref):
    context_len = qm_ref.shape[0]

    @pl.when(pl.program_id(0) == 0)
    def _():
        out_ref[...] = jnp.zeros_like(out_ref)
        sums_ref[:, :128] = jnp.ones((2, 128, context_len), jnp.bfloat16)
        sums_ref[:, 128:] = jnp.zeros((2, 128, context_len), jnp.bfloat16)

    line = lax.broadcasted_iota(jnp.int32, (16, context_len), 0)
    for g in range(2):
        u = u_ref[0, g : g + 1, :]
        high_part = u.astype(jnp.bfloat16).astype(jnp.float32)
        parts = jnp.where(line == 0, high_part, jnp.where(line == 1, u - high_part, 0.0))
        sums_ref[g, 128:144] = parts.astype(jnp.bfloat16)
    span = span_ref[0]
    for tb in range(context_len // block):
        low, high = tb * block, (tb + 1) * block

        @pl.when(span > low)
        def _():
            query = jnp.concatenate([qm_ref[low:high], qo_ref[low:high]], axis=1)
            t = lax.broadcasted_iota(jnp.int32, (block, high), 0) + low
            p = lax.broadcasted_iota(jnp.int32, (block, high), 1)
            allowed = (p <= t) & (p < jnp.maximum(span, 1))
            total = jnp.zeros((block, 128), jnp.float32)
            for g in range(2):
                score = lax.dot_general(
                    query, key_ref[0, g, :high], NT, preferred_element_type=jnp.float32
                )
                score = jnp.where(allowed, score, -jnp.inf)
                top = jnp.max(score, axis=-1, keepdims=True)
                grown = jnp.exp2((score - top) * (SCALE * math.log2(math.e))).astype(jnp.bfloat16)
                both = lax.dot_general(
                    grown, sums_ref[g, :, :high], NT, preferred_element_type=jnp.float32
                )
                total += both[:, 128:] / both[:, :128]
            out_ref[low:high] += total


def verify_call(span, q_mine, q_other, keys, u_pairs):
    context_len = q_mine.shape[0]
    pairs = u_pairs.shape[0]
    per_head = pairs // keys.shape[0]
    return pl.pallas_call(
        functools.partial(verify_kernel, min(256, context_len)),
        out_shape=jax.ShapeDtypeStruct((context_len, 128), jnp.float32),
        grid_spec=pltpu.PrefetchScalarGridSpec(
            num_scalar_prefetch=1,
            grid=(pairs,),
            in_specs=[
                pl.BlockSpec((context_len, 128), lambda i, s: (0, i)),
                pl.BlockSpec((context_len, 128), lambda i, s: (0, i)),
                pl.BlockSpec((1,) + keys.shape[1:], lambda i, s: (i // per_head, 0, 0, 0)),
                pl.BlockSpec((1, 2, context_len), lambda i, s: (i, 0, 0)),
            ],
            out_specs=pl.BlockSpec((context_len, 128), lambda i, s: (0, 0)),
            scratch_shapes=[pltpu.VMEM((2, 256, context_len), jnp.bfloat16)],
        ),
        compiler_params=pltpu.CompilerParams(vmem_limit_bytes=24 << 20),
        cost_estimate=pl.CostEstimate(
            flops=pairs * 8 * context_len * context_len * D_HEAD,
            bytes_accessed=8 << 20,
            transcendentals=pairs * context_len * context_len,
        ),
    )(span, q_mine, q_other, keys, u_pairs)


def body(kv_cache, new_kv, queries, verify_q, prompt_kv, readout, finish, dest, prompt, lengths):
    row_count, context_len, columns = kv_cache.shape
    step_count = new_kv.shape[0]
    slot_count = verify_q.shape[0]
    plen = prompt_kv.shape[1]
    kv_local = columns // (2 * HALF)
    tp_size = lax.axis_size("tensor")
    peer_count = lax.axis_size("dp")
    my_index = lax.axis_index("dp")
    side = lax.axis_index("tensor") // (tp_size // 2)
    pair_bit = tp_size.bit_length() - 2
    swap = functools.partial(from_partner, axis="tensor", apart=pair_bit)
    first_row = my_index * row_count
    per_side = slot_count // 2
    early = context_len // 2
    keep_query = lax.dynamic_slice_in_dim(verify_q, side * per_side, per_side)
    give_query = lax.dynamic_slice_in_dim(verify_q, (1 - side) * per_side, per_side)
    early_query = swap(give_query[:, :early])
    queries, lengths, give_query = lax.optimization_barrier((queries, lengths, give_query))
    my_length = lax.dynamic_slice_in_dim(lengths, first_row, row_count)

    half = row_count // 2
    step_queries = step_count * GROUP
    q_rows = queries.reshape(step_count, row_count, kv_local, GROUP, HALF)
    q_rows = q_rows.transpose(1, 2, 0, 3, 4).reshape(row_count, kv_local, step_queries, HALF)
    q_rows = jnp.pad(q_rows, ((0, 0), (0, 0), (0, 0), (0, HALF)))
    keep_meta = jnp.concatenate([(side * half)[None], my_length]).astype(jnp.int32)
    give_meta = jnp.concatenate([((1 - side) * half)[None], my_length]).astype(jnp.int32)
    flops = 2 * half * kv_local * step_queries * context_len * D_HEAD
    score_kind = jax.ShapeDtypeStruct((half, kv_local, step_queries, context_len), jnp.float32)
    weight_kind = jax.ShapeDtypeStruct(score_kind.shape, jnp.bfloat16)
    mixed_kind = jax.ShapeDtypeStruct((half, kv_local, step_queries, D_HEAD), jnp.float32)
    fresh = jnp.pad(new_kv.transpose(1, 0, 2), ((0, 0), (0, 16 - step_count), (0, 0)))
    (given,) = row_call(
        functools.partial(partial_kernel, kv_local, step_count),
        give_meta, (q_rows, kv_cache, fresh), ("all", "all", "all"), [score_kind], half, flops,
    )

    given, kv_cache, new_kv, fresh, finish, dest, prompt, readout = lax.optimization_barrier(
        (given, kv_cache, new_kv, fresh, finish, dest, prompt, readout)
    )
    other_part = swap(given)
    my_finish = lax.dynamic_slice_in_dim(finish, first_row, row_count)
    my_dest = lax.dynamic_slice_in_dim(dest, first_row, row_count)
    my_prompt = lax.dynamic_slice_in_dim(prompt, first_row, row_count)
    position = jnp.arange(context_len)

    finished_row = my_finish < step_count
    rank = jnp.cumsum(finished_row.astype(jnp.int32)) - 1
    weight = readout.reshape(kv_local, GROUP, HALF)
    target = jnp.where(finished_row, my_dest // slot_count, -1)
    turns = [finished_row & (rank == turn) for turn in range(2)]
    rows = jnp.stack([jnp.argmax(turn) for turn in turns]).astype(jnp.int32)
    goes = [jnp.max(jnp.where(turn, target, -1)) for turn in turns]
    picks = [(turn, jnp.maximum(my_prompt[rows[i]], 0)) for i, turn in enumerate(turns)]
    column = jnp.arange(columns)
    key_place = column // D_HEAD * HALF + column % HALF
    pick_keys = (key_place[:, None] == jnp.arange(columns // 2)[None, :]) & (
        column % D_HEAD < HALF
    )[:, None]
    keys, u_parts = pick_call(
        kv_local, step_count, jnp.concatenate([rows, my_length[rows]]), kv_cache, fresh,
        pick_keys.astype(jnp.bfloat16), jnp.pad(weight, ((0, 0), (0, 0), (HALF, 0))),
    )
    peers = jnp.arange(peer_count)[:, None, None]
    key_out = jnp.where(peers == goes[0], keys[:1], jnp.where(peers == goes[1], keys[1:], 0))
    u_out = jnp.where(peers == goes[0], u_parts[:1], jnp.where(peers == goes[1], u_parts[1:], 0.0))
    key_in = lax.all_to_all(key_out, "dp", split_axis=0, concat_axis=0, tiled=True)
    u_in = lax.all_to_all(u_out, "dp", split_axis=0, concat_axis=0, tiled=True)
    grown = kv_cache
    for step in range(step_count):
        hit = position[None, :] == my_length[:, None] + step
        grown = jnp.where(hit[:, :, None], new_kv[step][:, None, :], grown)

    wanted = my_index * slot_count + jnp.arange(slot_count)
    slot_hits = dest.reshape(peer_count, row_count)[None] == wanted[:, None, None]
    full_span = (lengths + finish + 1).reshape(peer_count, row_count)
    span_len = jnp.sum(jnp.where(slot_hits, full_span[None], 0), axis=(1, 2))
    source = jnp.argmax(jnp.any(slot_hits, axis=2), axis=1)

    def of_slots(array, first):
        return jnp.stack([
            lax.dynamic_index_in_dim(array, source[first + i], 0, keepdims=False)
            for i in range(per_side)
        ])

    first_keep, first_give = side * per_side, (1 - side) * per_side
    give_keys, give_u, other_part, grown, early_query, give_query = lax.optimization_barrier((
        of_slots(key_in, first_give), of_slots(u_in, first_give),
        other_part, grown, early_query, give_query,
    ))
    other_keys, other_u = swap((give_keys, give_u))
    other_query = swap(give_query[:, early:])
    keep_keys = of_slots(key_in, first_keep)

    prompts = lax.all_gather(prompt_kv, "dp", axis=0, tiled=True)
    other_part, prompts, cache = lax.optimization_barrier((other_part, prompts, grown))
    weights, mixed_keep = row_call(
        functools.partial(soft_kernel, kv_local),
        keep_meta, (q_rows, grown, other_part), ("all", "all", "half"),
        [weight_kind, mixed_kind], half, 2 * flops,
    )
    other_weights = swap(weights)
    other_query, weights, other_keys, other_u = lax.optimization_barrier(
        (other_query, weights, other_keys, other_u)
    )
    other_query = jnp.concatenate([early_query, other_query], axis=1)

    u_full = of_slots(u_in, first_keep) + other_u

    def by_head(keys):
        return keys.reshape(per_side, context_len, kv_local, HALF).transpose(0, 2, 1, 3)

    mine, other = by_head(keep_keys), by_head(other_keys)
    blank = jnp.zeros_like(mine)
    key_pairs = jnp.stack([
        jnp.concatenate([mine, blank, other, blank], axis=-1),
        jnp.concatenate([blank, mine, blank, other], axis=-1),
    ], axis=2)

    slot_rewards = []
    for i in range(per_side):
        slot_span = span_len[first_keep + i]
        reward = verify_call(
            slot_span[None].astype(jnp.int32), keep_query[i], other_query[i], key_pairs[i],
            u_full[i].reshape(kv_local * GROUP // 2, 2, context_len),
        )[:, :2].sum(axis=1)
        slot_rewards.append(jnp.where(position < slot_span, reward, 0.0))
    kept = jnp.stack(slot_rewards)
    shard = context_len // tp_size
    at = lax.axis_index("tensor")
    mine_sum = jnp.zeros((slot_count, shard), jnp.float32)
    for shift in range(tp_size):
        ring = [(z, (z + shift) % tp_size) for z in range(tp_size)]
        to_z = lax.rem(at + shift, tp_size)
        piece = lax.dynamic_slice_in_dim(kept, to_z * shard, shard, axis=1)
        if shift:
            piece = lax.ppermute(piece, "tensor", ring)
        from_side = lax.rem(at - shift + tp_size, tp_size) // (tp_size // 2)
        slots = jnp.arange(slot_count)[:, None] // per_side == from_side
        mine_sum += jnp.where(slots, jnp.tile(piece, (slot_count // per_side, 1)), 0.0)
    rewards = mine_sum

    (mixed_give,) = row_call(
        functools.partial(value_kernel, kv_local),
        give_meta, (other_weights, grown), ("half", "all"), [mixed_kind], half, flops,
    )
    mixed_keep, mixed_give = mixed_keep[..., HALF:], mixed_give[..., HALF:]
    mixed = jnp.concatenate([
        jnp.where(side == 0, mixed_keep, mixed_give), jnp.where(side == 0, mixed_give, mixed_keep)
    ]).reshape(row_count, kv_local, step_count, GROUP, HALF).transpose(2, 0, 1, 3, 4)
    live = jnp.arange(step_count)[:, None] <= my_finish[None, :]
    decoded = jnp.where(live[:, :, None, None, None], mixed, 0.0)
    decoded = decoded.astype(jnp.bfloat16).reshape(queries.shape)

    new_cache = cache
    for is_turn, which in picks:
        refill = lax.dynamic_index_in_dim(prompts, which, 0, keepdims=False)
        refill = jnp.pad(refill, ((0, context_len - plen), (0, 0)))
        new_cache = jnp.where(is_turn[:, None, None], refill[None], new_cache)
    return (decoded, new_cache, rewards)


def solution(mesh):
    placed = (
        P("dp", None, "tensor"),
        P(None, "dp", "tensor"),
        P(None, "dp", "tensor"),
        P("dp", None, "tensor"),
        P("dp", None, "tensor"),
        P("tensor"),
        P(),
        P(),
        P(),
        P(),
    )
    return jax.shard_map(
        body,
        mesh=mesh,
        in_specs=placed,
        out_specs=(P(None, "dp", "tensor"), P("dp", None, "tensor"), P("dp", "tensor")),
        check_vma=False,
    )
```

```python
import functools
import math

import jax
import jax.numpy as jnp
from jax import lax
from jax.experimental import pallas as pl
from jax.experimental.pallas import tpu as pltpu
from jax.sharding import PartitionSpec as P

GROUP = 8
D_HEAD = 128
HALF = 64
SCALE = 1.0 / math.sqrt(D_HEAD)
NT = (((1,), (1,)), ((), ()))


def from_partner(value, axis, apart):
    mask = 2**apart
    pairs = [(source, source ^ mask) for source in range(lax.axis_size(axis))]
    return lax.ppermute(value, axis, pairs)


def partial_kernel(heads, steps, meta_ref, q_ref, kv_ref, new_ref, out_ref):
    length = meta_ref[1 + meta_ref[0] + pl.program_id(0)]
    position = lax.broadcasted_iota(jnp.int32, out_ref.shape[2:], 1)
    for h in range(heads):
        tile = kv_ref[0, :, h * D_HEAD : (h + 1) * D_HEAD]
        fresh = new_ref[0, :, h * D_HEAD : (h + 1) * D_HEAD]
        score = lax.dot_general(q_ref[0, h], tile, NT, preferred_element_type=jnp.float32)
        extra = lax.dot_general(q_ref[0, h], fresh, NT, preferred_element_type=jnp.float32)
        for t in range(steps):
            score = jnp.where(position == length + t, extra[:, t : t + 1], score)
        out_ref[0, h] = score


def soft_kernel(heads, meta_ref, q_ref, kv_ref, other_ref, weight_ref, out_ref):
    row = meta_ref[0] + pl.program_id(0)
    length = meta_ref[1 + row]
    shape = other_ref.shape[2:]
    step = lax.broadcasted_iota(jnp.int32, shape, 0) // GROUP
    seen = lax.broadcasted_iota(jnp.int32, shape, 1) <= length + step
    for h in range(heads):
        tile = kv_ref[0, :, h * D_HEAD : (h + 1) * D_HEAD]
        mine = lax.dot_general(q_ref[0, h], tile, NT, preferred_element_type=jnp.float32)
        score = jnp.where(seen, (mine + other_ref[0, h]) * SCALE, -jnp.inf)
        score = jnp.exp(score - jnp.max(score, axis=-1, keepdims=True))
        weight = (score / jnp.sum(score, axis=-1, keepdims=True)).astype(jnp.bfloat16)
        weight_ref[0, h] = weight
        out_ref[0, h] = jnp.dot(weight, tile, preferred_element_type=jnp.float32)


def value_kernel(heads, meta_ref, weight_ref, kv_ref, out_ref):
    del meta_ref
    for h in range(heads):
        tile = kv_ref[0, :, h * D_HEAD : (h + 1) * D_HEAD]
        out_ref[0, h] = jnp.dot(weight_ref[0, h], tile, preferred_element_type=jnp.float32)


def row_call(kernel, meta, operands, kinds, out_kinds, rows, flops):
    def spec(shape, kind):
        tail = (0,) * (len(shape) - 1)
        if kind == "all":
            return pl.BlockSpec((1,) + shape[1:], lambda i, meta: (meta[0] + i,) + tail)
        return pl.BlockSpec((1,) + shape[1:], lambda i, meta: (i,) + tail)

    return pl.pallas_call(
        kernel,
        out_shape=out_kinds,
        grid_spec=pltpu.PrefetchScalarGridSpec(
            num_scalar_prefetch=1,
            grid=(rows,),
            in_specs=[spec(x.shape, k) for x, k in zip(operands, kinds)],
            out_specs=[spec(x.shape, "half") for x in out_kinds],
        ),
        cost_estimate=pl.CostEstimate(flops=flops, bytes_accessed=4 << 20, transcendentals=1 << 18),
    )(meta, *operands)


def pick_kernel(heads, steps, meta_ref, kv_ref, new_ref, pick_ref, weight_ref, key_ref, u_ref):
    length = meta_ref[2 + pl.program_id(0)]
    position = lax.broadcasted_iota(jnp.int32, key_ref.shape[1:], 0)
    keys = jnp.dot(kv_ref[0], pick_ref[...], preferred_element_type=jnp.float32)
    fresh = jnp.dot(new_ref[0], pick_ref[...], preferred_element_type=jnp.float32)
    for t in range(steps):
        keys = jnp.where(position == length + t, fresh[t : t + 1], keys)
    key_ref[0] = keys.astype(jnp.bfloat16)
    position = lax.broadcasted_iota(jnp.int32, (GROUP, u_ref.shape[2]), 1)
    for h in range(heads):
        at = slice(h * D_HEAD, (h + 1) * D_HEAD)
        u = lax.dot_general(weight_ref[h], kv_ref[0, :, at], NT, preferred_element_type=jnp.float32)
        extra = lax.dot_general(
            weight_ref[h], new_ref[0, :, at], NT, preferred_element_type=jnp.float32
        )
        for t in range(steps):
            u = jnp.where(position == length + t, extra[:, t : t + 1], u)
        u_ref[0, h * GROUP : (h + 1) * GROUP] = u


def pick_call(heads, steps, meta, kv, fresh, picks, weight):
    count, context_len, columns = kv.shape
    kinds = [
        jax.ShapeDtypeStruct((2, context_len, columns // 2), jnp.bfloat16),
        jax.ShapeDtypeStruct((2, heads * GROUP, context_len), jnp.float32),
    ]
    return pl.pallas_call(
        functools.partial(pick_kernel, heads, steps),
        out_shape=kinds,
        grid_spec=pltpu.PrefetchScalarGridSpec(
            num_scalar_prefetch=1,
            grid=(2,),
            in_specs=[
                pl.BlockSpec((1,) + kv.shape[1:], lambda i, meta: (meta[i], 0, 0)),
                pl.BlockSpec((1,) + fresh.shape[1:], lambda i, meta: (meta[i], 0, 0)),
                pl.BlockSpec(picks.shape, lambda i, meta: (0, 0)),
                pl.BlockSpec(weight.shape, lambda i, meta: (0, 0, 0)),
            ],
            out_specs=[pl.BlockSpec((1,) + k.shape[1:], lambda i, meta: (i, 0, 0)) for k in kinds],
        ),
        cost_estimate=pl.CostEstimate(flops=1 << 28, bytes_accessed=2 << 20, transcendentals=0),
    )(meta, kv, fresh, picks, weight)


def verify_kernel(block, span_ref, qm_ref, qo_ref, key_ref, u_ref, out_ref, sums_ref):
    context_len = qm_ref.shape[0]

    @pl.when(pl.program_id(0) == 0)
    def _():
        out_ref[...] = jnp.zeros_like(out_ref)
        sums_ref[:, :128] = jnp.ones((2, 128, context_len), jnp.bfloat16)
        sums_ref[:, 128:] = jnp.zeros((2, 128, context_len), jnp.bfloat16)

    line = lax.broadcasted_iota(jnp.int32, (16, context_len), 0)
    for g in range(2):
        u = u_ref[0, g : g + 1, :]
        high_part = u.astype(jnp.bfloat16).astype(jnp.float32)
        parts = jnp.where(line == 0, high_part, jnp.where(line == 1, u - high_part, 0.0))
        sums_ref[g, 128:144] = parts.astype(jnp.bfloat16)
    span = span_ref[0]
    for tb in range(context_len // block):
        low, high = tb * block, (tb + 1) * block

        @pl.when(span > low)
        def _():
            query = jnp.concatenate([qm_ref[low:high], qo_ref[low:high]], axis=1)
            t = lax.broadcasted_iota(jnp.int32, (block, high), 0) + low
            p = lax.broadcasted_iota(jnp.int32, (block, high), 1)
            allowed = (p <= t) & (p < jnp.maximum(span, 1))
            total = jnp.zeros((block, 128), jnp.float32)
            for g in range(2):
                score = lax.dot_general(
                    query, key_ref[0, g, :high], NT, preferred_element_type=jnp.float32
                )
                score = jnp.where(allowed, score, -jnp.inf)
                top = jnp.max(score, axis=-1, keepdims=True)
                grown = jnp.exp2((score - top) * (SCALE * math.log2(math.e))).astype(jnp.bfloat16)
                both = lax.dot_general(
                    grown, sums_ref[g, :, :high], NT, preferred_element_type=jnp.float32
                )
                total += both[:, 128:] / both[:, :128]
            out_ref[low:high] += total


def verify_call(span, q_mine, q_other, keys, u_pairs):
    context_len = q_mine.shape[0]
    pairs = u_pairs.shape[0]
    per_head = pairs // keys.shape[0]
    return pl.pallas_call(
        functools.partial(verify_kernel, min(256, context_len)),
        out_shape=jax.ShapeDtypeStruct((context_len, 128), jnp.float32),
        grid_spec=pltpu.PrefetchScalarGridSpec(
            num_scalar_prefetch=1,
            grid=(pairs,),
            in_specs=[
                pl.BlockSpec((context_len, 128), lambda i, s: (0, i)),
                pl.BlockSpec((context_len, 128), lambda i, s: (0, i)),
                pl.BlockSpec((1,) + keys.shape[1:], lambda i, s: (i // per_head, 0, 0, 0)),
                pl.BlockSpec((1, 2, context_len), lambda i, s: (i, 0, 0)),
            ],
            out_specs=pl.BlockSpec((context_len, 128), lambda i, s: (0, 0)),
            scratch_shapes=[pltpu.VMEM((2, 256, context_len), jnp.bfloat16)],
        ),
        compiler_params=pltpu.CompilerParams(vmem_limit_bytes=24 << 20),
        cost_estimate=pl.CostEstimate(
            flops=pairs * 8 * context_len * context_len * D_HEAD,
            bytes_accessed=8 << 20,
            transcendentals=pairs * context_len * context_len,
        ),
    )(span, q_mine, q_other, keys, u_pairs)


def body(kv_cache, new_kv, queries, verify_q, prompt_kv, readout, finish, dest, prompt, lengths):
    row_count, context_len, columns = kv_cache.shape
    step_count = new_kv.shape[0]
    slot_count = verify_q.shape[0]
    plen = prompt_kv.shape[1]
    kv_local = columns // (2 * HALF)
    tp_size = lax.axis_size("tensor")
    peer_count = lax.axis_size("dp")
    my_index = lax.axis_index("dp")
    side = lax.axis_index("tensor") // (tp_size // 2)
    pair_bit = tp_size.bit_length() - 2
    swap = functools.partial(from_partner, axis="tensor", apart=pair_bit)
    first_row = my_index * row_count
    per_side = slot_count // 2
    early = context_len * 3 // 4
    keep_query = lax.dynamic_slice_in_dim(verify_q, side * per_side, per_side)
    give_query = lax.dynamic_slice_in_dim(verify_q, (1 - side) * per_side, per_side)
    early_query = swap(give_query[:, :early])
    queries, lengths, give_query = lax.optimization_barrier((queries, lengths, give_query))
    my_length = lax.dynamic_slice_in_dim(lengths, first_row, row_count)

    half = row_count // 2
    step_queries = step_count * GROUP
    q_rows = queries.reshape(step_count, row_count, kv_local, GROUP, HALF)
    q_rows = q_rows.transpose(1, 2, 0, 3, 4).reshape(row_count, kv_local, step_queries, HALF)
    q_rows = jnp.pad(q_rows, ((0, 0), (0, 0), (0, 0), (0, HALF)))
    keep_meta = jnp.concatenate([(side * half)[None], my_length]).astype(jnp.int32)
    give_meta = jnp.concatenate([((1 - side) * half)[None], my_length]).astype(jnp.int32)
    flops = 2 * half * kv_local * step_queries * context_len * D_HEAD
    score_kind = jax.ShapeDtypeStruct((half, kv_local, step_queries, context_len), jnp.float32)
    weight_kind = jax.ShapeDtypeStruct(score_kind.shape, jnp.bfloat16)
    mixed_kind = jax.ShapeDtypeStruct((half, kv_local, step_queries, D_HEAD), jnp.float32)
    fresh = jnp.pad(new_kv.transpose(1, 0, 2), ((0, 0), (0, 16 - step_count), (0, 0)))
    (given,) = row_call(
        functools.partial(partial_kernel, kv_local, step_count),
        give_meta, (q_rows, kv_cache, fresh), ("all", "all", "all"), [score_kind], half, flops,
    )

    given, kv_cache, new_kv, fresh, finish, dest, prompt, readout = lax.optimization_barrier(
        (given, kv_cache, new_kv, fresh, finish, dest, prompt, readout)
    )
    other_part = swap(given)
    my_finish = lax.dynamic_slice_in_dim(finish, first_row, row_count)
    my_dest = lax.dynamic_slice_in_dim(dest, first_row, row_count)
    my_prompt = lax.dynamic_slice_in_dim(prompt, first_row, row_count)
    position = jnp.arange(context_len)

    finished_row = my_finish < step_count
    rank = jnp.cumsum(finished_row.astype(jnp.int32)) - 1
    weight = readout.reshape(kv_local, GROUP, HALF)
    target = jnp.where(finished_row, my_dest // slot_count, -1)
    turns = [finished_row & (rank == turn) for turn in range(2)]
    rows = jnp.stack([jnp.argmax(turn) for turn in turns]).astype(jnp.int32)
    goes = [jnp.max(jnp.where(turn, target, -1)) for turn in turns]
    picks = [(turn, jnp.maximum(my_prompt[rows[i]], 0)) for i, turn in enumerate(turns)]
    column = jnp.arange(columns)
    key_place = column // D_HEAD * HALF + column % HALF
    pick_keys = (key_place[:, None] == jnp.arange(columns // 2)[None, :]) & (
        column % D_HEAD < HALF
    )[:, None]
    keys, u_parts = pick_call(
        kv_local, step_count, jnp.concatenate([rows, my_length[rows]]), kv_cache, fresh,
        pick_keys.astype(jnp.bfloat16), jnp.pad(weight, ((0, 0), (0, 0), (HALF, 0))),
    )
    peers = jnp.arange(peer_count)[:, None, None]
    key_out = jnp.where(peers == goes[0], keys[:1], jnp.where(peers == goes[1], keys[1:], 0))
    u_out = jnp.where(peers == goes[0], u_parts[:1], jnp.where(peers == goes[1], u_parts[1:], 0.0))
    key_in = lax.all_to_all(key_out, "dp", split_axis=0, concat_axis=0, tiled=True)
    u_in = lax.all_to_all(u_out, "dp", split_axis=0, concat_axis=0, tiled=True)
    grown = kv_cache
    for step in range(step_count):
        hit = position[None, :] == my_length[:, None] + step
        grown = jnp.where(hit[:, :, None], new_kv[step][:, None, :], grown)

    wanted = my_index * slot_count + jnp.arange(slot_count)
    slot_hits = dest.reshape(peer_count, row_count)[None] == wanted[:, None, None]
    full_span = (lengths + finish + 1).reshape(peer_count, row_count)
    span_len = jnp.sum(jnp.where(slot_hits, full_span[None], 0), axis=(1, 2))
    source = jnp.argmax(jnp.any(slot_hits, axis=2), axis=1)

    def of_slots(array, first):
        return jnp.stack([
            lax.dynamic_index_in_dim(array, source[first + i], 0, keepdims=False)
            for i in range(per_side)
        ])

    first_keep, first_give = side * per_side, (1 - side) * per_side
    give_keys, give_u, other_part, grown, early_query, give_query = lax.optimization_barrier((
        of_slots(key_in, first_give), of_slots(u_in, first_give),
        other_part, grown, early_query, give_query,
    ))
    other_keys, other_u = swap((give_keys, give_u))
    other_query = swap(give_query[:, early:])
    keep_keys = of_slots(key_in, first_keep)

    prompts = lax.all_gather(prompt_kv, "dp", axis=0, tiled=True)
    other_part, prompts, cache = lax.optimization_barrier((other_part, prompts, grown))
    weights, mixed_keep = row_call(
        functools.partial(soft_kernel, kv_local),
        keep_meta, (q_rows, grown, other_part), ("all", "all", "half"),
        [weight_kind, mixed_kind], half, 2 * flops,
    )
    other_weights = swap(weights)
    other_query, weights, other_keys, other_u = lax.optimization_barrier(
        (other_query, weights, other_keys, other_u)
    )
    other_query = jnp.concatenate([early_query, other_query], axis=1)

    u_full = of_slots(u_in, first_keep) + other_u

    def by_head(keys):
        return keys.reshape(per_side, context_len, kv_local, HALF).transpose(0, 2, 1, 3)

    mine, other = by_head(keep_keys), by_head(other_keys)
    blank = jnp.zeros_like(mine)
    key_pairs = jnp.stack([
        jnp.concatenate([mine, blank, other, blank], axis=-1),
        jnp.concatenate([blank, mine, blank, other], axis=-1),
    ], axis=2)

    slot_rewards = []
    for i in range(per_side):
        slot_span = span_len[first_keep + i]
        reward = verify_call(
            slot_span[None].astype(jnp.int32), keep_query[i], other_query[i], key_pairs[i],
            u_full[i].reshape(kv_local * GROUP // 2, 2, context_len),
        )[:, :2].sum(axis=1)
        slot_rewards.append(jnp.where(position < slot_span, reward, 0.0))
    kept = jnp.stack(slot_rewards)
    shard = context_len // tp_size
    at = lax.axis_index("tensor")
    mine_sum = jnp.zeros((slot_count, shard), jnp.float32)
    for shift in range(tp_size):
        ring = [(z, (z + shift) % tp_size) for z in range(tp_size)]
        to_z = lax.rem(at + shift, tp_size)
        piece = lax.dynamic_slice_in_dim(kept, to_z * shard, shard, axis=1)
        if shift:
            piece = lax.ppermute(piece, "tensor", ring)
        from_side = lax.rem(at - shift + tp_size, tp_size) // (tp_size // 2)
        slots = jnp.arange(slot_count)[:, None] // per_side == from_side
        mine_sum += jnp.where(slots, jnp.tile(piece, (slot_count // per_side, 1)), 0.0)
    rewards = mine_sum

    (mixed_give,) = row_call(
        functools.partial(value_kernel, kv_local),
        give_meta, (other_weights, grown), ("half", "all"), [mixed_kind], half, flops,
    )
    mixed_keep, mixed_give = mixed_keep[..., HALF:], mixed_give[..., HALF:]
    mixed = jnp.concatenate([
        jnp.where(side == 0, mixed_keep, mixed_give), jnp.where(side == 0, mixed_give, mixed_keep)
    ]).reshape(row_count, kv_local, step_count, GROUP, HALF).transpose(2, 0, 1, 3, 4)
    live = jnp.arange(step_count)[:, None] <= my_finish[None, :]
    decoded = jnp.where(live[:, :, None, None, None], mixed, 0.0)
    decoded = decoded.astype(jnp.bfloat16).reshape(queries.shape)

    new_cache = cache
    for is_turn, which in picks:
        refill = lax.dynamic_index_in_dim(prompts, which, 0, keepdims=False)
        refill = jnp.pad(refill, ((0, context_len - plen), (0, 0)))
        new_cache = jnp.where(is_turn[:, None, None], refill[None], new_cache)
    return (decoded, new_cache, rewards)


def solution(mesh):
    placed = (
        P("dp", None, "tensor"),
        P(None, "dp", "tensor"),
        P(None, "dp", "tensor"),
        P("dp", None, "tensor"),
        P("dp", None, "tensor"),
        P("tensor"),
        P(),
        P(),
        P(),
        P(),
    )
    return jax.shard_map(
        body,
        mesh=mesh,
        in_specs=placed,
        out_specs=(P(None, "dp", "tensor"), P("dp", None, "tensor"), P("dp", "tensor")),
        check_vma=False,
    )
```
